32 devices in a mesh: req: 4 (over y, core), unit: 8 (over z, x).
Axes of the slice: x: 2, y: 2, z: 4, core: 2. Of those that a mesh axis runs over, the one named last changes fastest.
Arguments:
- hidden: bfloat16 [1536, 2048], P(('req', 'unit')), may hold values from -6 to 6
- tree_q: bfloat16 [1536, 2048], P(('req', 'unit')), may hold values from -1.5 to 1.5
- tree_kv: bfloat16 [1536, 2, 512], P(('req', 'unit')), may hold values from -1.5 to 1.5
- kv_cache: bfloat16 [32, 2, 2, 2048, 256], P(('req', 'unit')), may hold values from -1.5 to 1.5
- cache_lengths: int32 [32], P(('req', 'unit')), may hold values from 1 to 2048, as said below
- tree_parents: int32 [32, 48], P(('req', 'unit')), may hold values from 0 to 46, as said below
- accepted: int32 [32, 4], P(('req', 'unit')), may hold values from 0 to 47, as said below
- tenant_ranges: int32 [32, 2], replicated, may hold values from 0 to 262144, as said below
- out_weight: bfloat16 [2048, 2048], P(None, 'unit'), may hold values from -0.125 to 0.125
- mlp_weights: bfloat16 [3, 2048, 8192], P(None, None, ('req', 'unit')), may hold values from -0.125 to 0.125
- draft_weights: bfloat16 [4, 2048, 2048], P(None, None, 'unit'), may hold values from -0.125 to 0.125
- embedding: bfloat16 [262144, 2048], P(('req', 'unit')), may hold values from -1.1269514 to 1.1269514
- attn_post_gain: bfloat16 [2048], replicated, may hold values from 0.25 to 1.75
- ff_pre_gain: bfloat16 [2048], replicated, may hold values from 0.25 to 1.75
- ff_post_gain: bfloat16 [2048], replicated, may hold values from 0.25 to 1.75
- final_gain: bfloat16 [2048], replicated, may hold values from 0.25 to 1.75
Outputs:
- tree_out: bfloat16 [1536, 2048], P(('req', 'unit'))
- draft_logprobs: bfloat16 [4, 128, 262144], P(None, None, ('req', 'unit'))
The draws below stay inside these ranges and needn't reach their ends.
Inputs may be any that keep to these rules, and one draw needn't show every extreme that they name: A request's cache holds live entries in its first cache_lengths slots; some request fills all 2048. `tree_parents`: node 0 is the root and its own parent; every other node's parent has a smaller index. `accepted`: rising nodes starting at the root 0, each the parent of the next. `tenant_ranges`: column 0 is the first allowed id, column 1 one past the last; each request allows 262144 // 2 ids or more; some request allows all.
All inputs are finite; a program needn't handle non-finite values.
Results may differ from the reference program's by a relative error of at most 0.008.
Values may be sent and summed in bfloat16 or wider, within the bound.
A program may use at most 128 MiB of HBM per device.

```python
import math
import jax
import jax.numpy as jnp
from jax import lax

D = 2048
QH = 8
KVH = 2
HD = 256
FF = 8192
V = 262144
HEADS = 4
TREE = 48
ACC = 4
CACHE = 2048
REQUESTS = 32
TOKENS = 1536


def tree_shapes(key):
    base_key = jax.random.fold_in(key, 7)
    request_keys = jax.random.split(base_key, REQUESTS)

    def one_request(request_key):
        parent_key, path_key = jax.random.split(request_key)
        node_ids = jnp.arange(TREE, dtype=jnp.int32)
        parents = jax.random.randint(parent_key, (TREE,), 0, jnp.maximum(node_ids, 1))
        chosen = jnp.sort(jax.random.permutation(path_key, TREE - 1)[:ACC - 1] + 1)
        path_nodes = jnp.concatenate([jnp.zeros((1,), jnp.int32), chosen.astype(jnp.int32)])
        parents = parents.at[path_nodes[1:]].set(path_nodes[:-1])
        return (parents.astype(jnp.int32), path_nodes.astype(jnp.int32))
    return jax.vmap(one_request)(request_keys)


def draw_tree_parents(key, part):
    return tree_shapes(key)[0]


def draw_accepted(key, part):
    return tree_shapes(key)[1]


def draw_cache_lengths(key, part):
    first_key, second_key = jax.random.split(jax.random.fold_in(key, 3))
    lengths = jax.random.randint(first_key, (REQUESTS,), 1, CACHE // 2 + 1)
    longest = jax.random.randint(second_key, (), 0, REQUESTS)
    return lengths.at[longest].set(CACHE).astype(jnp.int32)


def draw_tenant_ranges(key, part):
    span_key, start_key, full_key = jax.random.split(jax.random.fold_in(key, 5), 3)
    spans = jax.random.randint(span_key, (REQUESTS,), V // 2, V + 1)
    starts = jax.random.randint(start_key, (REQUESTS,), 0, V - spans + 1)
    widest = jax.random.randint(full_key, (), 0, REQUESTS)
    spans = spans.at[widest].set(V)
    starts = starts.at[widest].set(0)
    return jnp.stack([starts, starts + spans], axis=1).astype(jnp.int32)


def draw_embedding(key, part):
    first_key, second_key = jax.random.split(jax.random.fold_in(key, 11))
    vocab_pos = jnp.arange(V, dtype=jnp.float32)[:, None]
    rising = 1.0 + 2.0 * vocab_pos / V
    spread = jnp.exp(jax.random.uniform(second_key, (V, 1), minval=math.log(0.7), maxval=math.log(1.4)))
    base = jnp.clip(jax.random.normal(first_key, (V, D)), -4.0, 4.0)
    return (base * rising * spread * (3.0 / math.sqrt(D))).astype(jnp.bfloat16)


def level_of(rng, shape, cuts, least, top_value):
    level, own = 1.0, jax.random.fold_in(rng, 6)
    for position, blocks in cuts:
        steps = jnp.exp(jax.random.uniform(jax.random.fold_in(own, position), (blocks,), jnp.float32, least / len(cuts), top_value / len(cuts)))
        level = level * jnp.repeat(steps, shape[position] // blocks).reshape([-1 if axis == position else 1 for axis in range(len(shape))])
    return level


def bell_draw(rng, shape, scale, limit, shards=(), kind=jnp.bfloat16):
    values = jax.random.normal(rng, shape, jnp.float32) * scale
    if len(shards) > 0:
        values = level_of(rng, shape, shards, -0.22, 0.18) * values
    return jnp.clip(values, min=-limit, max=limit).astype(kind)


def setup_inputs(seed: int = 0) -> dict:
    keys = jax.random.split(jax.random.key(seed), 17)
    return {
        "hidden": bell_draw(keys[0], (TOKENS, D), 1.0, 6.0, ((0, 32),)),
        "tree_q": jnp.clip(jax.random.uniform(keys[1], (TOKENS, QH * HD), jnp.float32, -1.5, 1.5) * level_of(keys[1], (TOKENS, QH * HD), ((0, 32),), -0.4, 0.0), -1.5, 1.5).astype(jnp.bfloat16),
        "tree_kv": jnp.clip(jax.random.uniform(keys[2], (TOKENS, 2, KVH * HD), jnp.float32, -1.5, 1.5) * level_of(keys[2], (TOKENS, 2, KVH * HD), ((0, 32),), -0.4, 0.0), -1.5, 1.5).astype(jnp.bfloat16),
        "kv_cache": jnp.clip(jax.random.uniform(keys[3], (REQUESTS, 2, KVH, CACHE, HD), jnp.float32, -1.5, 1.5) * level_of(keys[3], (REQUESTS, 2, KVH, CACHE, HD), ((0, 32),), -0.4, 0.0), -1.5, 1.5).astype(jnp.bfloat16),
        "cache_lengths": draw_cache_lengths(jax.random.fold_in(keys[16], 71), 0),
        "tree_parents": draw_tree_parents(jax.random.fold_in(keys[16], 71), 0),
        "accepted": draw_accepted(jax.random.fold_in(keys[16], 71), 0),
        "tenant_ranges": draw_tenant_ranges(jax.random.fold_in(keys[16], 71), 0),
        "out_weight": bell_draw(keys[8], (QH * HD, D), (QH * HD) ** -0.5, 0.125, ((1, 8),)),
        "mlp_weights": bell_draw(keys[9], (3, D, FF), D ** -0.5, 0.125, ((2, 32),)),
        "draft_weights": bell_draw(keys[10], (HEADS, D, D), D ** -0.5, 0.125, ((2, 8),)),
        "embedding": draw_embedding(jax.random.fold_in(keys[16], 71), 0),
        "attn_post_gain": jnp.clip(1.0 + 0.15 * jax.random.normal(keys[12], (D,), jnp.float32), 0.25, 1.75).astype(jnp.bfloat16),
        "ff_pre_gain": jnp.clip(1.0 + 0.15 * jax.random.normal(keys[13], (D,), jnp.float32), 0.25, 1.75).astype(jnp.bfloat16),
        "ff_post_gain": jnp.clip(1.0 + 0.15 * jax.random.normal(keys[14], (D,), jnp.float32), 0.25, 1.75).astype(jnp.bfloat16),
        "final_gain": jnp.clip(1.0 + 0.15 * jax.random.normal(keys[15], (D,), jnp.float32), 0.25, 1.75).astype(jnp.bfloat16),
    }


EPS = 1e-06
SOFTCAP = 30.0

def rms_scale(values, gain):
    floats = values.astype(jnp.float32)
    return floats * lax.rsqrt(lax.optimization_barrier(jnp.mean(floats * floats, axis=-1, keepdims=True)) + EPS) * gain.astype(jnp.float32)

def ancestor_table(parents):
    tree_size = parents.shape[-1]
    node_ids = jnp.arange(tree_size, dtype=jnp.int32)
    reachable = jnp.maximum((parents[:, None] == node_ids[None, :]).astype(jnp.float32), (node_ids[:, None] == node_ids[None, :]).astype(jnp.float32))
    for doubling in range(max(1, (tree_size - 1).bit_length())):
        reachable = jnp.minimum(jnp.dot(reachable, reachable, precision=lax.Precision.HIGHEST), 1.0)
    return reachable

def rounded_weights(values):
    return lax.optimization_barrier(values.astype(jnp.bfloat16)).astype(jnp.float32)

def attend_request(query, tree_pairs, cache, length, parents):
    tree_size = query.shape[0]
    group_size = QH // KVH
    score_scale = HD ** (-0.5)
    queries = query.astype(jnp.float32).reshape(tree_size, KVH, group_size, HD)
    cache_keys = cache[0].astype(jnp.float32)
    cache_values = cache[1].astype(jnp.float32)
    cache_scores = jnp.exp(jnp.einsum('tkgd,ksd->kgts', queries, cache_keys) * score_scale)
    slot_ids = jnp.arange(CACHE, dtype=jnp.int32)
    cache_probs = jnp.where(slot_ids < length, cache_scores, 0.0)
    tree_keys = tree_pairs[:, 0].astype(jnp.float32).reshape(tree_size, KVH, HD)
    tree_values = tree_pairs[:, 1].astype(jnp.float32).reshape(tree_size, KVH, HD)
    tree_scores = jnp.exp(jnp.einsum('tkgd,skd->kgts', queries, tree_keys) * score_scale)
    tree_probs = tree_scores * ancestor_table(parents)
    denominator = lax.optimization_barrier(jnp.sum(cache_probs, axis=3)) + lax.optimization_barrier(jnp.sum(tree_probs, axis=3))
    numerator = jnp.einsum('kgts,ksd->tkgd', rounded_weights(cache_probs), cache_values)
    numerator = numerator + jnp.einsum('kgts,skd->tkgd', rounded_weights(tree_probs), tree_values)
    result = numerator / jnp.transpose(denominator, (2, 0, 1))[..., None]
    return result.reshape(tree_size, QH * HD).astype(jnp.bfloat16)

def reference(hidden, tree_q, tree_kv, kv_cache, cache_lengths, tree_parents, accepted, tenant_ranges, out_weight, mlp_weights, draft_weights, embedding, attn_post_gain, ff_pre_gain, ff_post_gain, final_gain):
    queries = tree_q.reshape(REQUESTS, TREE, QH * HD)
    tree_pairs = tree_kv.reshape(REQUESTS, TREE, 2, KVH * HD)
    attended = lax.map(lambda items: attend_request(*items), (queries, tree_pairs, kv_cache, cache_lengths, tree_parents))
    attended = attended.reshape(TOKENS, QH * HD)
    projected = jnp.dot(attended, out_weight, preferred_element_type=jnp.float32).astype(jnp.bfloat16)
    first = (hidden.astype(jnp.float32) + rms_scale(projected, attn_post_gain)).astype(jnp.bfloat16)
    normed = rms_scale(first, ff_pre_gain).astype(jnp.bfloat16)
    gate_part = jnp.dot(normed, mlp_weights[0], preferred_element_type=jnp.float32)
    upward = jnp.dot(normed, mlp_weights[1], preferred_element_type=jnp.float32)
    active = (jax.nn.gelu(gate_part, approximate=True) * upward).astype(jnp.bfloat16)
    mlp_sum = lax.dot_general(active, mlp_weights[2], (((1,), (1,)), ((), ())), preferred_element_type=jnp.float32)
    tree_out = (first.astype(jnp.float32) + rms_scale(mlp_sum, ff_post_gain)).astype(jnp.bfloat16)
    row_ids = (jnp.arange(REQUESTS, dtype=jnp.int32)[:, None] * TREE + accepted).reshape(-1)
    path_rows = tree_out[row_ids]
    path_normed = rms_scale(path_rows, final_gain).astype(jnp.bfloat16)
    before = jnp.einsum('rd,hde->rhe', path_normed.astype(jnp.float32), draft_weights.astype(jnp.float32))
    drafts = (path_normed.astype(jnp.float32)[:, None, :] + jax.nn.silu(before)).astype(jnp.bfloat16)
    starts = jnp.repeat(tenant_ranges[:, 0], ACC)
    range_ends = jnp.repeat(tenant_ranges[:, 1], ACC)
    vocab_ids = jnp.arange(V, dtype=jnp.int32)
    allowed = (vocab_ids[None, :] >= starts[:, None]) & (vocab_ids[None, :] < range_ends[:, None])

    def one_head(head_rows):
        logits = SOFTCAP * jnp.tanh(jnp.dot(head_rows, embedding.T, preferred_element_type=jnp.float32) / SOFTCAP)
        totals = lax.optimization_barrier(jnp.sum(jnp.where(allowed, jnp.exp(logits), 0.0), axis=1, keepdims=True))
        return jnp.where(allowed, logits - jnp.log(totals), 0.0).astype(jnp.bfloat16)
    draft_logprobs = lax.map(one_head, jnp.transpose(drafts, (1, 0, 2)))
    return (tree_out, draft_logprobs)
```

```python
import functools

import jax
import jax.numpy as jnp
from jax import lax
from jax.experimental import pallas as pl
from jax.experimental.pallas import tpu as pltpu
from jax.sharding import PartitionSpec as P

QH = 8
KVH = 2
HD = 256
HEADS = 4
ACC = 4

EPS = 1e-06
SOFTCAP = 30.0
MIB = 1024 * 1024
NT = (((1,), (1,)), ((), ()))


def rms_scale(values, gain):
    floats = values.astype(jnp.float32)
    return (
        floats
        * lax.rsqrt(jnp.mean(floats * floats, axis=-1, keepdims=True) + EPS)
        * gain.astype(jnp.float32)
    )


def dot_nt(left, right):
    return lax.dot_general(left, right, NT, preferred_element_type=jnp.float32)


def attention_kernel(length_ref, parents_ref, q_ref, tk_ref, tv_ref, cache_ref, out_ref):
    tree = q_ref.shape[0]
    group = QH // KVH
    slots = cache_ref.shape[3]
    width = min(512, slots)
    scale = HD ** (-0.5)
    length = length_ref[0]
    node = lax.broadcasted_iota(jnp.int32, (tree, tree), 0)
    other = lax.broadcasted_iota(jnp.int32, (tree, tree), 1)
    eye = jnp.where(node == other, 1.0, 0.0)
    parent = jnp.broadcast_to(parents_ref[...], (tree, tree))
    below = jnp.maximum(jnp.where(parent == node, 1.0, 0.0), eye)
    for _ in range(max(1, (tree - 1).bit_length())):
        bits = below.astype(jnp.bfloat16)
        below = jnp.minimum(jnp.dot(bits, bits, preferred_element_type=jnp.float32), 1.0)
    ancestor = lax.dot_general(
        below.astype(jnp.bfloat16),
        eye.astype(jnp.bfloat16),
        (((0,), (0,)), ((), ())),
        preferred_element_type=jnp.float32,
    )
    queries = jnp.concatenate([q_ref[:, g * HD : (g + 1) * HD] for g in range(group)], axis=0)
    weights = jnp.exp(dot_nt(queries, tk_ref[...]) * scale) * jnp.concatenate([ancestor] * group, 0)
    total = jnp.sum(weights, axis=1, keepdims=True)
    number = jnp.dot(
        weights.astype(jnp.bfloat16), tv_ref[...], preferred_element_type=jnp.float32
    )
    for block in range(slots // width):
        span = slice(block * width, (block + 1) * width)
        scores = jnp.exp(dot_nt(queries, cache_ref[0, 0, 0, span, :]) * scale)
        slot = block * width + lax.broadcasted_iota(jnp.int32, scores.shape, 1)
        weights = jnp.where(slot < length, scores, 0.0)
        total = total + jnp.sum(weights, axis=1, keepdims=True)
        number = number + jnp.dot(
            weights.astype(jnp.bfloat16),
            cache_ref[0, 1, 0, span, :],
            preferred_element_type=jnp.float32,
        )
    result = (number / total).astype(jnp.bfloat16)
    for g in range(group):
        out_ref[:, g * HD : (g + 1) * HD] = result[g * tree : (g + 1) * tree, :]


def attend(tree_q, tree_kv, kv_cache, cache_lengths, tree_parents):
    tree = tree_q.shape[0]
    slots = kv_cache.shape[3]
    wide = QH // KVH * HD
    return pl.pallas_call(
        attention_kernel,
        grid=(KVH,),
        out_shape=jax.ShapeDtypeStruct((tree, QH * HD), jnp.bfloat16),
        in_specs=[
            pl.BlockSpec(memory_space=pltpu.SMEM),
            pl.BlockSpec((1, tree), lambda k: (0, 0)),
            pl.BlockSpec((tree, wide), lambda k: (0, k)),
            pl.BlockSpec((tree, HD), lambda k: (0, k)),
            pl.BlockSpec((tree, HD), lambda k: (0, k)),
            pl.BlockSpec((1, 2, 1, slots, HD), lambda k: (0, 0, k, 0, 0)),
        ],
        out_specs=pl.BlockSpec((tree, wide), lambda k: (0, k)),
        compiler_params=pltpu.CompilerParams(vmem_limit_bytes=24 * MIB),
        cost_estimate=pl.CostEstimate(
            flops=4 * tree * QH * HD * slots,
            bytes_accessed=8 * slots * KVH * HD,
            transcendentals=tree * QH * slots,
        ),
        name="tree_attention",
    )(cache_lengths, tree_parents, tree_q, tree_kv[:, 0], tree_kv[:, 1], kv_cache)


def draft_kernel(rows_ref, weight_ref, out_ref):
    width = weight_ref.shape[2]
    start = pl.multiple_of(lax.axis_index("unit") * width, width)
    before = jnp.dot(rows_ref[...], weight_ref[0], preferred_element_type=jnp.float32)
    own = rows_ref[:, pl.ds(start, width)].astype(jnp.float32)
    out_ref[0] = (own + before * jax.nn.sigmoid(before)).astype(jnp.bfloat16)


def draft_columns(rows, draft_weights):
    count, depth = rows.shape
    heads, _, width = draft_weights.shape
    return pl.pallas_call(
        draft_kernel,
        grid=(heads,),
        out_shape=jax.ShapeDtypeStruct((heads, count, width), jnp.bfloat16),
        in_specs=[
            pl.BlockSpec((count, depth), lambda h: (0, 0)),
            pl.BlockSpec((1, depth, width), lambda h: (h, 0, 0)),
        ],
        out_specs=pl.BlockSpec((1, count, width), lambda h: (h, 0, 0)),
        compiler_params=pltpu.CompilerParams(vmem_limit_bytes=24 * MIB),
        cost_estimate=pl.CostEstimate(
            flops=2 * heads * count * depth * width,
            bytes_accessed=2 * heads * depth * width,
            transcendentals=heads * count * width,
        ),
        name="draft_heads",
    )(rows, draft_weights)


def allowed_ids(start, end, first_id, shape):
    ids = first_id + lax.broadcasted_iota(jnp.int32, shape, 1)
    return (ids >= start) & (ids < end)


def logits_kernel(chunk, drafts_ref, emb_ref, start_ref, end_ref, logits_ref, sums_ref, rows_ref):
    step = pl.program_id(0)
    blocks, count, width = drafts_ref.shape
    tile = emb_ref.shape[0]
    vocab = tile * pl.num_programs(0)
    first_id = (lax.axis_index("req") * lax.axis_size("unit") + lax.axis_index("unit")) * vocab

    @pl.when(step == 0)
    def _():
        for b in range(blocks):
            rows_ref[:, b * width : (b + 1) * width] = drafts_ref[b]
        sums_ref[...] = jnp.zeros_like(sums_ref)

    start, end = start_ref[...], end_ref[...]
    for c in range(tile // chunk):
        span = slice(c * chunk, (c + 1) * chunk)
        products = dot_nt(rows_ref[...], emb_ref[span, :])
        logits = SOFTCAP * jnp.tanh(products * (1.0 / SOFTCAP))
        logits_ref[:, span] = logits
        keep = allowed_ids(start, end, first_id + step * tile + c * chunk, logits.shape)
        terms = jnp.where(keep, jnp.exp(logits), 0.0)
        part = terms[:, :128]
        for lane in range(128, chunk, 128):
            part = part + terms[:, lane : lane + 128]
        sums_ref[...] += part


def finish_kernel(logits_ref, logs_ref, start_ref, end_ref, out_ref):
    tile = logits_ref.shape[1]
    vocab = tile * pl.num_programs(0)
    first_id = (lax.axis_index("req") * lax.axis_size("unit") + lax.axis_index("unit")) * vocab
    keep = allowed_ids(
        start_ref[...], end_ref[...], first_id + pl.program_id(0) * tile, logits_ref.shape
    )
    values = jnp.where(keep, logits_ref[...] - logs_ref[...], 0.0).astype(jnp.bfloat16)
    out_ref[...] = values.reshape(out_ref.shape)


def vocabulary(drafts, embedding, tenant_ranges):
    blocks, count, width = drafts.shape
    vocab, depth = embedding.shape
    rows = count // HEADS
    bounds = jnp.tile(jnp.repeat(tenant_ranges, ACC, axis=0), (HEADS, 1))
    starts, ends = bounds[:, :1], bounds[:, 1:]
    tile = min(1024, vocab, MIB // 2 // count)
    once = pl.BlockSpec((count, 1), lambda i: (0, 0))
    logits, sums = pl.pallas_call(
        functools.partial(logits_kernel, min(256, tile)),
        grid=(vocab // tile,),
        out_shape=(
            jax.ShapeDtypeStruct((count, vocab), jnp.float32),
            jax.ShapeDtypeStruct((count, 128), jnp.float32),
        ),
        in_specs=[
            pl.BlockSpec((blocks, count, width), lambda i: (0, 0, 0)),
            pl.BlockSpec((tile, depth), lambda i: (i, 0)),
            once,
            once,
        ],
        out_specs=(
            pl.BlockSpec((count, tile), lambda i: (0, i)),
            pl.BlockSpec((count, 128), lambda i: (0, 0)),
        ),
        scratch_shapes=[pltpu.VMEM((count, depth), jnp.bfloat16)],
        compiler_params=pltpu.CompilerParams(vmem_limit_bytes=56 * MIB),
        cost_estimate=pl.CostEstimate(
            flops=2 * count * depth * vocab,
            bytes_accessed=2 * depth * vocab + 4 * count * vocab,
            transcendentals=2 * count * vocab,
        ),
        name="vocabulary_logits",
    )(drafts, embedding, starts, ends)
    totals = lax.psum(jnp.sum(sums, axis=1), ("req", "unit"))
    return pl.pallas_call(
        finish_kernel,
        grid=(vocab // tile,),
        out_shape=jax.ShapeDtypeStruct((HEADS, rows, vocab), jnp.bfloat16),
        in_specs=[pl.BlockSpec((count, tile), lambda i: (0, i)), once, once, once],
        out_specs=pl.BlockSpec((HEADS, rows, tile), lambda i: (0, 0, i)),
        compiler_params=pltpu.CompilerParams(vmem_limit_bytes=40 * MIB),
        cost_estimate=pl.CostEstimate(
            flops=2 * count * vocab, bytes_accessed=6 * count * vocab, transcendentals=0
        ),
        name="log_probabilities",
    )(logits, jnp.log(totals)[:, None], starts, ends)


def unit_terms(mlp_rows, weight_part):
    gate_part = jnp.dot(mlp_rows, weight_part[0], preferred_element_type=jnp.float32)
    upward = jnp.dot(mlp_rows, weight_part[1], preferred_element_type=jnp.float32)
    active = (jax.nn.gelu(gate_part, approximate=True) * upward).astype(jnp.bfloat16)
    return dot_nt(active, weight_part[2])


def project_rows(attended, out_weight):
    cols = jnp.dot(
        lax.all_gather(attended, "unit", axis=0, tiled=True),
        out_weight,
        preferred_element_type=jnp.float32,
    ).astype(jnp.bfloat16)
    return lax.all_to_all(cols, "unit", split_axis=0, concat_axis=1, tiled=True)


def per_device(
    hidden,
    tree_q,
    tree_kv,
    kv_cache,
    cache_lengths,
    tree_parents,
    accepted,
    tenant_ranges,
    out_weight,
    mlp_weights,
    draft_weights,
    embedding,
    attn_post_gain,
    ff_pre_gain,
    ff_post_gain,
    final_gain,
):
    group_weights = lax.all_gather(mlp_weights, "req", axis=2, tiled=True)
    attended = attend(tree_q, tree_kv, kv_cache, cache_lengths, tree_parents)

    def after_attention(residual, projected):
        first = (residual.astype(jnp.float32) + rms_scale(projected, attn_post_gain)).astype(
            jnp.bfloat16
        )
        return first, rms_scale(first, ff_pre_gain).astype(jnp.bfloat16)

    def after_mlp(first, mlp_sum):
        return (first.astype(jnp.float32) + rms_scale(mlp_sum, ff_post_gain)).astype(jnp.bfloat16)

    path_attended = jnp.take(attended, accepted[0], axis=0)
    path_hidden = jnp.take(hidden, accepted[0], axis=0)
    path_first, path_mlp_rows = after_attention(
        path_hidden, project_rows(path_attended, out_weight)
    )
    partial = unit_terms(
        lax.all_gather(path_mlp_rows, ("req", "unit"), axis=0, tiled=True), mlp_weights
    )
    path_sum = lax.psum_scatter(partial, ("req", "unit"), scatter_dimension=0, tiled=True)
    path_normed = rms_scale(after_mlp(path_first, path_sum), final_gain).astype(jnp.bfloat16)
    every_row = lax.all_gather(path_normed, ("req", "unit"), axis=0, tiled=True)
    own = draft_columns(every_row, draft_weights)
    own = own.reshape(own.shape[0] * own.shape[1], own.shape[2])
    drafts = lax.all_gather(own, "unit", axis=0)
    draft_logprobs = vocabulary(drafts, embedding, tenant_ranges)

    first, normed = after_attention(hidden, project_rows(attended, out_weight))
    mlp_rows = lax.all_gather(normed, "unit", axis=0, tiled=True)
    partial_sums = unit_terms(mlp_rows, group_weights)
    mlp_sum = lax.psum_scatter(partial_sums, "unit", scatter_dimension=0, tiled=True)
    return (after_mlp(first, mlp_sum), draft_logprobs)


def solution(mesh):
    return jax.shard_map(
        per_device,
        mesh=mesh,
        in_specs=(
            P(("req", "unit"), None),
            P(("req", "unit"), None),
            P(("req", "unit"), None, None),
            P(("req", "unit"), None, None, None, None),
            P(("req", "unit")),
            P(("req", "unit"), None),
            P(("req", "unit"), None),
            P(),
            P(None, "unit"),
            P(None, None, ("req", "unit")),
            P(None, None, "unit"),
            P(("req", "unit"), None),
            P(),
            P(),
            P(),
            P(),
        ),
        out_specs=(P(("req", "unit"), None), P(None, None, ("req", "unit"))),
        check_vma=False,
    )
```

```python
import functools

import jax
import jax.numpy as jnp
from jax import lax
from jax.experimental import pallas as pl
from jax.experimental.pallas import tpu as pltpu
from jax.sharding import PartitionSpec as P

QH = 8
KVH = 2
HD = 256
HEADS = 4
ACC = 4

EPS = 1e-06
SOFTCAP = 30.0
MIB = 1024 * 1024
NT = (((1,), (1,)), ((), ()))
MESH = pl.DeviceIdType.MESH
PACK = 16 // ACC


def rms_scale(values, gain):
    floats = values.astype(jnp.float32)
    return (
        floats
        * lax.rsqrt(jnp.mean(floats * floats, axis=-1, keepdims=True) + EPS)
        * gain.astype(jnp.float32)
    )


def dot_nt(left, right):
    return lax.dot_general(left, right, NT, preferred_element_type=jnp.float32)


def attention_kernel(length_ref, parents_ref, q_ref, tk_ref, tv_ref, cache_ref, out_ref):
    tree = q_ref.shape[0]
    group = QH // KVH
    slots = cache_ref.shape[3]
    width = min(512, slots)
    scale = HD ** (-0.5)
    length = length_ref[0]
    node = lax.broadcasted_iota(jnp.int32, (tree, tree), 0)
    other = lax.broadcasted_iota(jnp.int32, (tree, tree), 1)
    eye = jnp.where(node == other, 1.0, 0.0)
    parent = jnp.broadcast_to(parents_ref[...], (tree, tree))
    below = jnp.maximum(jnp.where(parent == node, 1.0, 0.0), eye)
    for _ in range(max(1, (tree - 1).bit_length())):
        bits = below.astype(jnp.bfloat16)
        below = jnp.minimum(jnp.dot(bits, bits, preferred_element_type=jnp.float32), 1.0)
    ancestor = lax.dot_general(
        below.astype(jnp.bfloat16),
        eye.astype(jnp.bfloat16),
        (((0,), (0,)), ((), ())),
        preferred_element_type=jnp.float32,
    )
    queries = jnp.concatenate([q_ref[:, g * HD : (g + 1) * HD] for g in range(group)], axis=0)
    weights = jnp.exp(dot_nt(queries, tk_ref[...]) * scale) * jnp.concatenate([ancestor] * group, 0)
    total = jnp.sum(weights, axis=1, keepdims=True)
    number = jnp.dot(
        weights.astype(jnp.bfloat16), tv_ref[...], preferred_element_type=jnp.float32
    )
    for block in range(slots // width):
        span = slice(block * width, (block + 1) * width)
        scores = jnp.exp(dot_nt(queries, cache_ref[0, 0, 0, span, :]) * scale)
        slot = block * width + lax.broadcasted_iota(jnp.int32, scores.shape, 1)
        weights = jnp.where(slot < length, scores, 0.0)
        total = total + jnp.sum(weights, axis=1, keepdims=True)
        number = number + jnp.dot(
            weights.astype(jnp.bfloat16),
            cache_ref[0, 1, 0, span, :],
            preferred_element_type=jnp.float32,
        )
    result = (number / total).astype(jnp.bfloat16)
    for g in range(group):
        out_ref[:, g * HD : (g + 1) * HD] = result[g * tree : (g + 1) * tree, :]


def attend(tree_q, tree_kv, kv_cache, cache_lengths, tree_parents):
    tree = tree_q.shape[0]
    slots = kv_cache.shape[3]
    wide = QH // KVH * HD
    return pl.pallas_call(
        attention_kernel,
        grid=(KVH,),
        out_shape=jax.ShapeDtypeStruct((tree, QH * HD), jnp.bfloat16),
        in_specs=[
            pl.BlockSpec(memory_space=pltpu.SMEM),
            pl.BlockSpec((1, tree), lambda k: (0, 0)),
            pl.BlockSpec((tree, wide), lambda k: (0, k)),
            pl.BlockSpec((tree, HD), lambda k: (0, k)),
            pl.BlockSpec((tree, HD), lambda k: (0, k)),
            pl.BlockSpec((1, 2, 1, slots, HD), lambda k: (0, 0, k, 0, 0)),
        ],
        out_specs=pl.BlockSpec((tree, wide), lambda k: (0, k)),
        compiler_params=pltpu.CompilerParams(vmem_limit_bytes=24 * MIB),
        cost_estimate=pl.CostEstimate(
            flops=4 * tree * QH * HD * slots,
            bytes_accessed=8 * slots * KVH * HD,
            transcendentals=tree * QH * slots,
        ),
        name="tree_attention",
    )(cache_lengths, tree_parents, tree_q, tree_kv[:, 0], tree_kv[:, 1], kv_cache)


def split_unit(size):
    fast = 2 ** ((size.bit_length() - 1) // 2)
    return size // fast, fast


class Place:
    def __init__(self):
        self.reqs, self.units = lax.axis_size("req"), lax.axis_size("unit")
        self.r, self.u = lax.axis_index("req"), lax.axis_index("unit")
        self.slow, self.fast = split_unit(self.units)
        self.z, self.x = self.u // self.fast, lax.rem(self.u, self.fast)
        self.chips, self.cores = self.reqs // 2, 2
        self.y, self.c = self.r // 2, lax.rem(self.r, 2)

    def unit(self, dz, dx):
        return lax.rem(self.z + dz, self.slow) * self.fast + lax.rem(self.x + dx, self.fast)

    def unit_from(self, dz, dx):
        return self.unit(self.slow - dz, self.fast - dx)

    def req(self, dy, dc):
        return lax.rem(self.y + dy, self.chips) * 2 + lax.rem(self.c + dc, 2)

    def req_from(self, dy, dc):
        return self.req(self.chips - dy, 2 - dc)

    def unit_peers(self):
        return [(dz, dx) for dz in range(self.slow) for dx in range(self.fast) if dz or dx]

    def req_peers(self):
        return [(dy, dc) for dy in range(self.chips) for dc in range(2) if dy or dc]


def meet(at):
    barrier = pltpu.get_barrier_semaphore()
    for dz, dx in at.unit_peers():
        pl.semaphore_signal(
            barrier, inc=1, device_id=(at.r, at.unit(dz, dx)), device_id_type=MESH
        )
    for dy, dc in at.req_peers():
        pl.semaphore_signal(barrier, inc=1, device_id=(at.req(dy, dc), at.u), device_id_type=MESH)
    pl.semaphore_wait(barrier, at.units + at.reqs - 2)


def push(src, dst, send, recv, r, u):
    copy = pltpu.make_async_remote_copy(
        src_ref=src,
        dst_ref=dst,
        send_sem=send,
        recv_sem=recv,
        device_id=(r, u),
        device_id_type=MESH,
    )
    copy.start()
    return copy


def await_block(at, ref, send, recv):
    pltpu.make_async_remote_copy(
        src_ref=ref,
        dst_ref=ref,
        send_sem=send,
        recv_sem=recv,
        device_id=(at.r, at.u),
        device_id_type=MESH,
    ).wait_recv()


def gather_units(at, own, buf, send, recv):
    sent = []
    for dz in range(1, at.slow):
        sent.append(
            push(own, buf.at[at.u], send.at[dz, 0], recv.at[at.u], at.r, at.unit(dz, 0))
        )
    for dx in range(1, at.fast):
        sent.append(
            push(own, buf.at[at.u], send.at[0, dx], recv.at[at.u], at.r, at.unit(0, dx))
        )
    buf[at.u] = own[...]
    for dz in range(1, at.slow):
        slot = at.unit_from(dz, 0)
        await_block(at, buf.at[slot], send.at[dz, 0], recv.at[slot])
        for dx in range(1, at.fast):
            sent.append(
                push(buf.at[slot], buf.at[slot], send.at[dz, dx], recv.at[slot], at.r, at.unit(0, dx))
            )
    for dz in range(at.slow):
        for dx in range(1, at.fast):
            slot = at.unit_from(dz, dx)
            await_block(at, buf.at[slot], send.at[dz, dx], recv.at[slot])
    return sent


def layer_kernel(
    accepted_ref,
    attended_ref,
    hidden_ref,
    out_weight_ref,
    attn_gain_ref,
    pre_gain_ref,
    post_gain_ref,
    final_gain_ref,
    mlp_ref,
    tree_out_ref,
    path_ref,
    weights,
    attended_all,
    proj_send,
    proj_recv,
    first_ref,
    normed_ref,
    normed_all,
    part,
    sums_send,
    sums_fast,
    sums_slow,
    own_sem,
    w_send,
    w_recv,
    a_send,
    a_recv,
    p_send,
    p_recv,
    n_send,
    n_recv,
    f_send,
    f_recv,
    s_send,
    s_recv,
):
    at = Place()
    units, tree, depth = attended_all.shape
    matrices = mlp_ref.shape[0]
    meet(at)

    own_copy = pltpu.make_async_copy(mlp_ref, weights.at[at.r], own_sem)
    own_copy.start()
    w_sent = []
    for m in range(matrices):
        for dy in range(1, at.chips):
            w_sent.append(
                push(
                    mlp_ref.at[m],
                    weights.at[at.r, m],
                    w_send.at[dy, 0, m],
                    w_recv.at[at.r, m],
                    at.req(dy, 0),
                    at.u,
                )
            )
        w_sent.append(
            push(
                mlp_ref.at[m],
                weights.at[at.r, m],
                w_send.at[0, 1, m],
                w_recv.at[at.r, m],
                at.req(0, 1),
                at.u,
            )
        )

    def pass_on(m):
        for dy in range(1, at.chips):
            slot = at.req_from(dy, 0)
            block = weights.at[slot, m]
            await_block(at, block, w_send.at[dy, 0, m], w_recv.at[slot, m])
            w_sent.append(
                push(block, block, w_send.at[dy, 1, m], w_recv.at[slot, m], at.req(0, 1), at.u)
            )

    sent = gather_units(at, attended_ref, attended_all, a_send, a_recv)
    columns = jnp.dot(
        attended_all[...].reshape(units * tree, depth),
        out_weight_ref[...],
        preferred_element_type=jnp.float32,
    ).astype(jnp.bfloat16)
    proj_send[...] = columns.reshape(proj_send.shape)
    for dz, dx in at.unit_peers():
        peer = at.unit(dz, dx)
        sent.append(
            push(
                proj_send.at[peer],
                proj_recv.at[at.u],
                p_send.at[dz, dx],
                p_recv.at[at.u],
                at.r,
                peer,
            )
        )
    proj_recv[at.u] = proj_send[at.u]
    for dz, dx in at.unit_peers():
        slot = at.unit_from(dz, dx)
        await_block(at, proj_recv.at[slot], p_send.at[dz, dx], p_recv.at[slot])
    projected = jnp.concatenate([proj_recv[j] for j in range(units)], axis=1)
    first = (
        hidden_ref[...].astype(jnp.float32) + rms_scale(projected, attn_gain_ref[...])
    ).astype(jnp.bfloat16)
    first_ref[...] = first
    normed_ref[...] = rms_scale(first, pre_gain_ref[...]).astype(jnp.bfloat16)
    pass_on(0)
    sent += gather_units(at, normed_ref, normed_all, n_send, n_recv)
    for m in range(1, matrices):
        pass_on(m)

    own_copy.wait()

    def add_units(slot, start):
        rows = normed_all[...].reshape(units * tree, depth)
        gate = jnp.dot(rows, weights[slot, 0], preferred_element_type=jnp.float32)
        upward = jnp.dot(rows, weights[slot, 1], preferred_element_type=jnp.float32)
        active = (jax.nn.gelu(gate, approximate=True) * upward).astype(jnp.bfloat16)
        terms = dot_nt(active, weights[slot, 2]).reshape(units, tree, depth)
        part[...] = terms if start else part[...] + terms

    add_units(at.r, True)

    def one_chip(dy, carry):
        @pl.when(dy > 0)
        def _():
            add_units(at.req_from(dy, 0), False)

        slot = at.req_from(dy, 1)
        for m in range(matrices):
            await_block(at, weights.at[slot, m], w_send.at[0, 1, m], w_recv.at[slot, m])
        add_units(slot, False)
        return carry

    lax.fori_loop(0, at.chips, one_chip, 0)

    order = list(range(1, at.slow)) + [0]
    for dz in order:
        for dx in range(1, at.fast):
            peer = at.unit(dz, dx)
            zt = peer // at.fast
            sums_send[peer] = part[peer].astype(jnp.bfloat16)
            sent.append(
                push(
                    sums_send.at[peer],
                    sums_fast.at[zt, at.x],
                    f_send.at[dz, dx],
                    f_recv.at[zt, at.x],
                    at.r,
                    at.unit(0, dx),
                )
            )
    for dz in order:
        target = at.unit(dz, 0)
        zt = target // at.fast
        total = part[target]
        for dx in range(1, at.fast):
            xs = lax.rem(at.x + at.fast - dx, at.fast)
            await_block(at, sums_fast.at[zt, xs], f_send.at[dz, dx], f_recv.at[zt, xs])
            total = total + sums_fast[zt, xs].astype(jnp.float32)
        if dz:
            sums_send[target] = total.astype(jnp.bfloat16)
            sent.append(
                push(
                    sums_send.at[target],
                    sums_slow.at[at.z],
                    s_send.at[dz],
                    s_recv.at[at.z],
                    at.r,
                    target,
                )
            )
    for dz in range(1, at.slow):
        zs = lax.rem(at.z + at.slow - dz, at.slow)
        await_block(at, sums_slow.at[zs], s_send.at[dz], s_recv.at[zs])
        total = total + sums_slow[zs].astype(jnp.float32)
    tree_out = (
        first_ref[...].astype(jnp.float32) + rms_scale(total, post_gain_ref[...])
    ).astype(jnp.bfloat16)
    tree_out_ref[...] = tree_out

    ready = rms_scale(tree_out, final_gain_ref[...]).astype(jnp.bfloat16)
    width = depth // PACK
    row = lax.broadcasted_iota(jnp.int32, (PACK * ACC, tree), 0)
    node = lax.broadcasted_iota(jnp.int32, (PACK * ACC, tree), 1)
    packed = jnp.zeros((PACK * ACC, width), jnp.float32)
    for chunk in range(PACK):
        pick = jnp.zeros((PACK * ACC, tree), jnp.float32)
        for i in range(ACC):
            hit = (row == chunk * ACC + i) & (node == accepted_ref[0, i])
            pick = jnp.where(hit, 1.0, pick)
        packed = packed + jnp.dot(
            pick.astype(jnp.bfloat16),
            ready[:, chunk * width : (chunk + 1) * width],
            preferred_element_type=jnp.float32,
        )
    path_ref[...] = packed.astype(jnp.bfloat16)
    for copy in sent + w_sent:
        copy.wait_send()


def layer(attended, hidden, accepted, out_weight, mlp_weights, gains):
    reqs, units = lax.axis_size("req"), lax.axis_size("unit")
    slow, fast = split_unit(units)
    tree, depth = hidden.shape
    bf16, dma = jnp.bfloat16, pltpu.SemaphoreType.DMA
    vmem = pl.BlockSpec(memory_space=pltpu.VMEM)
    rows = (units, tree, depth)
    cols = (units, tree, out_weight.shape[1])
    matrices, _, width = mlp_weights.shape
    return pl.pallas_call(
        layer_kernel,
        out_shape=(
            jax.ShapeDtypeStruct((tree, depth), bf16),
            jax.ShapeDtypeStruct((PACK * ACC, depth // PACK), bf16),
        ),
        in_specs=[pl.BlockSpec(memory_space=pltpu.SMEM)]
        + [vmem] * 7
        + [pl.BlockSpec(memory_space=pl.ANY)],
        out_specs=(vmem, vmem),
        scratch_shapes=[
            pltpu.VMEM((reqs, matrices, depth, width), bf16),
            pltpu.VMEM(rows, bf16),
            pltpu.VMEM(cols, bf16),
            pltpu.VMEM(cols, bf16),
            pltpu.VMEM((tree, depth), bf16),
            pltpu.VMEM((tree, depth), bf16),
            pltpu.VMEM(rows, bf16),
            pltpu.VMEM(rows, jnp.float32),
            pltpu.VMEM(rows, bf16),
            pltpu.VMEM((slow, fast, tree, depth), bf16),
            pltpu.VMEM((slow, tree, depth), bf16),
            dma(()),
            dma((reqs // 2, 2, matrices)),
            dma((reqs, matrices)),
            dma((slow, fast)),
            dma((units,)),
            dma((slow, fast)),
            dma((units,)),
            dma((slow, fast)),
            dma((units,)),
            dma((slow, fast)),
            dma((slow, fast)),
            dma((slow,)),
            dma((slow,)),
        ],
        compiler_params=pltpu.CompilerParams(
            collective_id=0, has_side_effects=True, vmem_limit_bytes=56 * MIB
        ),
        name="projection_and_feed_forward",
    )(accepted, attended, hidden, out_weight, *[g[None, :] for g in gains], mlp_weights)


def drafts_kernel(
    path_ref,
    weight_ref,
    out_ref,
    paths,
    every,
    weight,
    drafts,
    own_sem,
    l_send,
    l_recv,
    m_send,
    m_recv,
    a_send,
    a_recv,
    q_send,
    q_recv,
):
    at = Place()
    reqs, units, packed, wide = paths.shape
    heads = weight_ref.shape[0]
    rows, depth = every.shape
    share, width = drafts.shape[2:]
    head = at.r * heads // reqs
    load = pltpu.make_async_copy(weight_ref.at[head], weight, own_sem)
    load.start()
    meet(at)

    sent = []
    for dz, dx in at.unit_peers():
        sent.append(
            push(
                path_ref,
                paths.at[at.r, at.u],
                l_send.at[dz, dx],
                l_recv.at[at.u],
                at.r,
                at.unit(dz, dx),
            )
        )
    paths[at.r, at.u] = path_ref[...]
    for dz, dx in at.unit_peers():
        slot = at.unit_from(dz, dx)
        await_block(at, paths.at[at.r, slot], l_send.at[dz, dx], l_recv.at[slot])
    for dy, dc in at.req_peers():
        sent.append(
            push(
                paths.at[at.r],
                paths.at[at.r],
                m_send.at[dy, dc],
                m_recv.at[at.r],
                at.req(dy, dc),
                at.u,
            )
        )
    for dy, dc in at.req_peers():
        slot = at.req_from(dy, dc)
        await_block(at, paths.at[slot], m_send.at[dy, dc], m_recv.at[slot])
    flat = paths[...].reshape(reqs * units * packed, wide)
    row = lax.broadcasted_iota(jnp.int32, (rows, flat.shape[0]), 0)
    place = lax.broadcasted_iota(jnp.int32, (rows, flat.shape[0]), 1)
    base = row // ACC * packed + lax.rem(row, ACC)
    for chunk in range(PACK):
        pick = jnp.where(place == base + chunk * ACC, 1.0, 0.0).astype(jnp.bfloat16)
        every[:, chunk * wide : (chunk + 1) * wide] = jnp.dot(
            pick, flat, preferred_element_type=jnp.float32
        ).astype(jnp.bfloat16)

    load.wait()
    if share == rows:
        mine = every.at[:, :]
    else:
        start = pl.multiple_of(lax.rem(at.r * share, rows), share)
        mine = every.at[pl.ds(start, share), :]
    before = jnp.dot(mine[...], weight[...], preferred_element_type=jnp.float32)
    own = mine[:, pl.ds(pl.multiple_of(at.u * width, width), width)].astype(jnp.float32)
    drafts[at.r, at.u] = (own + before * jax.nn.sigmoid(before)).astype(jnp.bfloat16)

    block = drafts.at[at.r, at.u]
    for dz in range(1, at.slow):
        sent.append(push(block, block, a_send.at[dz, 0], a_recv.at[at.u], at.r, at.unit(dz, 0)))
    for dz in range(at.slow):
        slot = at.unit_from(dz, 0)
        block = drafts.at[at.r, slot]
        if dz:
            await_block(at, block, a_send.at[dz, 0], a_recv.at[slot])
        for dx in range(1, at.fast):
            sent.append(push(block, block, a_send.at[dz, dx], a_recv.at[slot], at.r, at.unit(0, dx)))
    for dz in range(at.slow):
        for dx in range(1, at.fast):
            slot = at.unit_from(dz, dx)
            await_block(at, drafts.at[at.r, slot], a_send.at[dz, dx], a_recv.at[slot])
    block = drafts.at[at.r]
    for dy in range(1, at.chips):
        sent.append(push(block, block, q_send.at[dy, 0], q_recv.at[at.r], at.req(dy, 0), at.u))
    for dy in range(at.chips):
        slot = at.req_from(dy, 0)
        block = drafts.at[slot]
        if dy:
            await_block(at, block, q_send.at[dy, 0], q_recv.at[slot])
        sent.append(push(block, block, q_send.at[dy, 1], q_recv.at[slot], at.req(0, 1), at.u))
    for dy in range(at.chips):
        slot = at.req_from(dy, 1)
        await_block(at, drafts.at[slot], q_send.at[dy, 1], q_recv.at[slot])
    for k in range(reqs):
        for j in range(units):
            out_ref[k * share : (k + 1) * share, j * width : (j + 1) * width] = drafts[k, j]
    for copy in sent:
        copy.wait_send()


def gather_drafts(path, draft_weights):
    reqs, units = lax.axis_size("req"), lax.axis_size("unit")
    slow, fast = split_unit(units)
    heads, depth, width = draft_weights.shape
    rows = reqs * units * ACC
    share = heads * rows // reqs
    bf16, dma = jnp.bfloat16, pltpu.SemaphoreType.DMA
    vmem = pl.BlockSpec(memory_space=pltpu.VMEM)
    return pl.pallas_call(
        drafts_kernel,
        out_shape=jax.ShapeDtypeStruct((heads * rows, depth), bf16),
        in_specs=[vmem, pl.BlockSpec(memory_space=pl.ANY)],
        out_specs=vmem,
        scratch_shapes=[
            pltpu.VMEM((reqs, units) + path.shape, bf16),
            pltpu.VMEM((rows, depth), bf16),
            pltpu.VMEM((depth, width), bf16),
            pltpu.VMEM((reqs, units, share, width), bf16),
            dma(()),
            dma((slow, fast)),
            dma((units,)),
            dma((reqs // 2, 2)),
            dma((reqs,)),
            dma((slow, fast)),
            dma((units,)),
            dma((reqs // 2, 2)),
            dma((reqs,)),
        ],
        compiler_params=pltpu.CompilerParams(
            collective_id=1, has_side_effects=True, vmem_limit_bytes=48 * MIB
        ),
        name="draft_heads",
    )(path, draft_weights)


def sum_kernel(own_ref, out_ref, unit_parts, group, req_parts, u_send, u_recv, r_send, r_recv):
    at = Place()
    meet(at)
    sent = []
    for dz, dx in at.unit_peers():
        sent.append(
            push(
                own_ref,
                unit_parts.at[at.u],
                u_send.at[dz, dx],
                u_recv.at[at.u],
                at.r,
                at.unit(dz, dx),
            )
        )
    unit_parts[at.u] = own_ref[...]
    for dz, dx in at.unit_peers():
        slot = at.unit_from(dz, dx)
        await_block(at, unit_parts.at[slot], u_send.at[dz, dx], u_recv.at[slot])
    group[...] = jnp.sum(unit_parts[...], axis=0)
    for dy, dc in at.req_peers():
        sent.append(
            push(
                group,
                req_parts.at[at.r],
                r_send.at[dy, dc],
                r_recv.at[at.r],
                at.req(dy, dc),
                at.u,
            )
        )
    req_parts[at.r] = group[...]
    for dy, dc in at.req_peers():
        slot = at.req_from(dy, dc)
        await_block(at, req_parts.at[slot], r_send.at[dy, dc], r_recv.at[slot])
    out_ref[...] = jnp.sum(req_parts[...], axis=0)
    for copy in sent:
        copy.wait_send()


def sum_over_devices(values):
    reqs, units = lax.axis_size("req"), lax.axis_size("unit")
    slow, fast = split_unit(units)
    lines = max(8, values.shape[0] // 128)
    block = (lines, 128)
    f32, dma = jnp.float32, pltpu.SemaphoreType.DMA
    vmem = pl.BlockSpec(memory_space=pltpu.VMEM)
    padded = jnp.pad(values, (0, lines * 128 - values.shape[0])).reshape(block)
    summed = pl.pallas_call(
        sum_kernel,
        out_shape=jax.ShapeDtypeStruct(block, f32),
        in_specs=[vmem],
        out_specs=vmem,
        scratch_shapes=[
            pltpu.VMEM((units,) + block, f32),
            pltpu.VMEM(block, f32),
            pltpu.VMEM((reqs,) + block, f32),
            dma((slow, fast)),
            dma((units,)),
            dma((reqs // 2, 2)),
            dma((reqs,)),
        ],
        compiler_params=pltpu.CompilerParams(collective_id=2, has_side_effects=True),
        name="sum_of_totals",
    )(padded)
    return summed.reshape(-1)[: values.shape[0]]


def allowed_ids(start, end, first_id, shape):
    ids = first_id + lax.broadcasted_iota(jnp.int32, shape, 1)
    return (ids >= start) & (ids < end)


def logits_kernel(chunk, drafts_ref, emb_ref, start_ref, end_ref, logits_ref, sums_ref):
    step = pl.program_id(0)
    count = drafts_ref.shape[0]
    tile = emb_ref.shape[0]
    vocab = tile * pl.num_programs(0)
    first_id = (lax.axis_index("req") * lax.axis_size("unit") + lax.axis_index("unit")) * vocab

    @pl.when(step == 0)
    def _():
        sums_ref[...] = jnp.zeros_like(sums_ref)

    start, end = start_ref[...], end_ref[...]
    for c in range(tile // chunk):
        span = slice(c * chunk, (c + 1) * chunk)
        products = dot_nt(drafts_ref[...], emb_ref[span, :])
        logits = SOFTCAP * jnp.tanh(products * (1.0 / SOFTCAP))
        logits_ref[:, span] = logits
        keep = allowed_ids(start, end, first_id + step * tile + c * chunk, logits.shape)
        terms = jnp.where(keep, jnp.exp(logits), 0.0)
        part = terms[:, :128]
        for lane in range(128, chunk, 128):
            part = part + terms[:, lane : lane + 128]
        sums_ref[...] += part


def finish_kernel(logits_ref, logs_ref, start_ref, end_ref, out_ref):
    tile = logits_ref.shape[1]
    vocab = tile * pl.num_programs(0)
    first_id = (lax.axis_index("req") * lax.axis_size("unit") + lax.axis_index("unit")) * vocab
    keep = allowed_ids(
        start_ref[...], end_ref[...], first_id + pl.program_id(0) * tile, logits_ref.shape
    )
    values = jnp.where(keep, logits_ref[...] - logs_ref[...], 0.0).astype(jnp.bfloat16)
    out_ref[...] = values.reshape(out_ref.shape)


def vocabulary(drafts, embedding, tenant_ranges):
    count = drafts.shape[0]
    vocab, depth = embedding.shape
    rows = count // HEADS
    bounds = jnp.tile(jnp.repeat(tenant_ranges, ACC, axis=0), (HEADS, 1))
    starts, ends = bounds[:, :1], bounds[:, 1:]
    tile = min(1024, vocab, MIB // 2 // count)
    once = pl.BlockSpec((count, 1), lambda i: (0, 0))
    logits, sums = pl.pallas_call(
        functools.partial(logits_kernel, min(256, tile)),
        grid=(vocab // tile,),
        out_shape=(
            jax.ShapeDtypeStruct((count, vocab), jnp.float32),
            jax.ShapeDtypeStruct((count, 128), jnp.float32),
        ),
        in_specs=[
            pl.BlockSpec((count, depth), lambda i: (0, 0)),
            pl.BlockSpec((tile, depth), lambda i: (i, 0)),
            once,
            once,
        ],
        out_specs=(
            pl.BlockSpec((count, tile), lambda i: (0, i)),
            pl.BlockSpec((count, 128), lambda i: (0, 0)),
        ),
        compiler_params=pltpu.CompilerParams(vmem_limit_bytes=56 * MIB),
        cost_estimate=pl.CostEstimate(
            flops=2 * count * depth * vocab,
            bytes_accessed=2 * depth * vocab + 4 * count * vocab,
            transcendentals=2 * count * vocab,
        ),
        name="vocabulary_logits",
    )(drafts, embedding, starts, ends)
    totals = sum_over_devices(jnp.sum(sums, axis=1))
    return pl.pallas_call(
        finish_kernel,
        grid=(vocab // tile,),
        out_shape=jax.ShapeDtypeStruct((HEADS, rows, vocab), jnp.bfloat16),
        in_specs=[pl.BlockSpec((count, tile), lambda i: (0, i)), once, once, once],
        out_specs=pl.BlockSpec((HEADS, rows, tile), lambda i: (0, 0, i)),
        compiler_params=pltpu.CompilerParams(vmem_limit_bytes=40 * MIB),
        cost_estimate=pl.CostEstimate(
            flops=2 * count * vocab, bytes_accessed=6 * count * vocab, transcendentals=0
        ),
        name="log_probabilities",
    )(logits, jnp.log(totals)[:, None], starts, ends)


def per_device(
    hidden,
    tree_q,
    tree_kv,
    kv_cache,
    cache_lengths,
    tree_parents,
    accepted,
    tenant_ranges,
    out_weight,
    mlp_weights,
    draft_weights,
    embedding,
    attn_post_gain,
    ff_pre_gain,
    ff_post_gain,
    final_gain,
):
    attended = attend(tree_q, tree_kv, kv_cache, cache_lengths, tree_parents)
    gains = (attn_post_gain, ff_pre_gain, ff_post_gain, final_gain)
    tree_out, path = layer(attended, hidden, accepted, out_weight, mlp_weights, gains)
    drafts = gather_drafts(path, draft_weights)
    return (tree_out, vocabulary(drafts, embedding, tenant_ranges))


def solution(mesh):
    return jax.shard_map(
        per_device,
        mesh=mesh,
        in_specs=(
            P(("req", "unit"), None),
            P(("req", "unit"), None),
            P(("req", "unit"), None, None),
            P(("req", "unit"), None, None, None, None),
            P(("req", "unit")),
            P(("req", "unit"), None),
            P(("req", "unit"), None),
            P(),
            P(None, "unit"),
            P(None, None, ("req", "unit")),
            P(None, None, "unit"),
            P(("req", "unit"), None),
            P(),
            P(),
            P(),
            P(),
        ),
        out_specs=(P(("req", "unit"), None), P(None, None, ("req", "unit"))),
        check_vma=False,
    )
```

```python
import functools

import jax
import jax.numpy as jnp
from jax import lax
from jax.experimental import pallas as pl
from jax.experimental.pallas import tpu as pltpu
from jax.sharding import PartitionSpec as P

QH = 8
KVH = 2
HD = 256
HEADS = 4
ACC = 4

EPS = 1e-06
SOFTCAP = 30.0
MIB = 1024 * 1024
NT = (((1,), (1,)), ((), ()))
MESH = pl.DeviceIdType.MESH
PACK = 16 // ACC


def rms_scale(values, gain):
    floats = values.astype(jnp.float32)
    return (
        floats
        * lax.rsqrt(jnp.mean(floats * floats, axis=-1, keepdims=True) + EPS)
        * gain.astype(jnp.float32)
    )


def dot_nt(left, right):
    return lax.dot_general(left, right, NT, preferred_element_type=jnp.float32)


def attention_kernel(length_ref, parents_ref, q_ref, tk_ref, tv_ref, cache_ref, out_ref):
    tree = q_ref.shape[0]
    group = QH // KVH
    slots = cache_ref.shape[3]
    width = min(512, slots)
    scale = HD ** (-0.5)
    length = length_ref[0]
    node = lax.broadcasted_iota(jnp.int32, (tree, tree), 0)
    other = lax.broadcasted_iota(jnp.int32, (tree, tree), 1)
    eye = jnp.where(node == other, 1.0, 0.0)
    parent = jnp.broadcast_to(parents_ref[...], (tree, tree))
    below = jnp.maximum(jnp.where(parent == node, 1.0, 0.0), eye)
    for _ in range(max(1, (tree - 1).bit_length())):
        bits = below.astype(jnp.bfloat16)
        below = jnp.minimum(jnp.dot(bits, bits, preferred_element_type=jnp.float32), 1.0)
    ancestor = lax.dot_general(
        below.astype(jnp.bfloat16),
        eye.astype(jnp.bfloat16),
        (((0,), (0,)), ((), ())),
        preferred_element_type=jnp.float32,
    )
    queries = jnp.concatenate([q_ref[:, g * HD : (g + 1) * HD] for g in range(group)], axis=0)
    weights = jnp.exp(dot_nt(queries, tk_ref[...]) * scale) * jnp.concatenate([ancestor] * group, 0)
    total = jnp.sum(weights, axis=1, keepdims=True)
    number = jnp.dot(
        weights.astype(jnp.bfloat16), tv_ref[...], preferred_element_type=jnp.float32
    )
    for block in range(slots // width):
        span = slice(block * width, (block + 1) * width)
        scores = jnp.exp(dot_nt(queries, cache_ref[0, 0, 0, span, :]) * scale)
        slot = block * width + lax.broadcasted_iota(jnp.int32, scores.shape, 1)
        weights = jnp.where(slot < length, scores, 0.0)
        total = total + jnp.sum(weights, axis=1, keepdims=True)
        number = number + jnp.dot(
            weights.astype(jnp.bfloat16),
            cache_ref[0, 1, 0, span, :],
            preferred_element_type=jnp.float32,
        )
    result = (number / total).astype(jnp.bfloat16)
    for g in range(group):
        out_ref[:, g * HD : (g + 1) * HD] = result[g * tree : (g + 1) * tree, :]


def attend(tree_q, tree_kv, kv_cache, cache_lengths, tree_parents):
    tree = tree_q.shape[0]
    slots = kv_cache.shape[3]
    wide = QH // KVH * HD
    return pl.pallas_call(
        attention_kernel,
        grid=(KVH,),
        out_shape=jax.ShapeDtypeStruct((tree, QH * HD), jnp.bfloat16),
        in_specs=[
            pl.BlockSpec(memory_space=pltpu.SMEM),
            pl.BlockSpec((1, tree), lambda k: (0, 0)),
            pl.BlockSpec((tree, wide), lambda k: (0, k)),
            pl.BlockSpec((tree, HD), lambda k: (0, k)),
            pl.BlockSpec((tree, HD), lambda k: (0, k)),
            pl.BlockSpec((1, 2, 1, slots, HD), lambda k: (0, 0, k, 0, 0)),
        ],
        out_specs=pl.BlockSpec((tree, wide), lambda k: (0, k)),
        compiler_params=pltpu.CompilerParams(vmem_limit_bytes=24 * MIB),
        cost_estimate=pl.CostEstimate(
            flops=4 * tree * QH * HD * slots,
            bytes_accessed=8 * slots * KVH * HD,
            transcendentals=tree * QH * slots,
        ),
        name="tree_attention",
    )(cache_lengths, tree_parents, tree_q, tree_kv[:, 0], tree_kv[:, 1], kv_cache)


def split_unit(size):
    fast = 2 ** ((size.bit_length() - 1) // 2)
    return size // fast, fast


class Place:
    def __init__(self):
        self.reqs, self.units = lax.axis_size("req"), lax.axis_size("unit")
        self.r, self.u = lax.axis_index("req"), lax.axis_index("unit")
        self.slow, self.fast = split_unit(self.units)
        self.z, self.x = self.u // self.fast, lax.rem(self.u, self.fast)
        self.chips, self.cores = self.reqs // 2, 2
        self.y, self.c = self.r // 2, lax.rem(self.r, 2)

    def unit(self, dz, dx):
        return lax.rem(self.z + dz, self.slow) * self.fast + lax.rem(self.x + dx, self.fast)

    def unit_from(self, dz, dx):
        return self.unit(self.slow - dz, self.fast - dx)

    def req(self, dy, dc):
        return lax.rem(self.y + dy, self.chips) * 2 + lax.rem(self.c + dc, 2)

    def req_from(self, dy, dc):
        return self.req(self.chips - dy, 2 - dc)

    def unit_peers(self):
        return [(dz, dx) for dz in range(self.slow) for dx in range(self.fast) if dz or dx]

    def req_peers(self):
        return [(dy, dc) for dy in range(self.chips) for dc in range(2) if dy or dc]


def meet(at):
    barrier = pltpu.get_barrier_semaphore()
    for dz, dx in at.unit_peers():
        pl.semaphore_signal(
            barrier, inc=1, device_id=(at.r, at.unit(dz, dx)), device_id_type=MESH
        )
    for dy, dc in at.req_peers():
        pl.semaphore_signal(barrier, inc=1, device_id=(at.req(dy, dc), at.u), device_id_type=MESH)
    pl.semaphore_wait(barrier, at.units + at.reqs - 2)


def push(src, dst, send, recv, r, u):
    copy = pltpu.make_async_remote_copy(
        src_ref=src,
        dst_ref=dst,
        send_sem=send,
        recv_sem=recv,
        device_id=(r, u),
        device_id_type=MESH,
    )
    copy.start()
    return copy


def await_block(at, ref, send, recv):
    pltpu.make_async_remote_copy(
        src_ref=ref,
        dst_ref=ref,
        send_sem=send,
        recv_sem=recv,
        device_id=(at.r, at.u),
        device_id_type=MESH,
    ).wait_recv()


def start_gather(at, own, buf, send, recv):
    sent = []
    for dz in range(1, at.slow):
        sent.append(
            push(own, buf.at[at.u], send.at[dz, 0], recv.at[at.u], at.r, at.unit(dz, 0))
        )
    for dx in range(1, at.fast):
        sent.append(
            push(own, buf.at[at.u], send.at[0, dx], recv.at[at.u], at.r, at.unit(0, dx))
        )
    buf[at.u] = own[...]
    return sent


def forward_gather(at, buf, send, recv):
    sent = []
    for dz in range(1, at.slow):
        slot = at.unit_from(dz, 0)
        await_block(at, buf.at[slot], send.at[dz, 0], recv.at[slot])
        for dx in range(1, at.fast):
            sent.append(
                push(buf.at[slot], buf.at[slot], send.at[dz, dx], recv.at[slot], at.r, at.unit(0, dx))
            )
    return sent


def end_gather(at, buf, send, recv):
    for dz in range(at.slow):
        for dx in range(1, at.fast):
            slot = at.unit_from(dz, dx)
            await_block(at, buf.at[slot], send.at[dz, dx], recv.at[slot])


def start_packed(at, own, buf, send, recv):
    sent = []
    for dz, dx in at.unit_peers():
        sent.append(
            push(own, buf.at[at.r, at.u], send.at[dz, dx], recv.at[at.u], at.r, at.unit(dz, dx))
        )
    buf[at.r, at.u] = own[...]
    return sent


def spread_packed(at, buf, l_send, l_recv, m_send, m_recv):
    sent = []
    for dz, dx in at.unit_peers():
        slot = at.unit_from(dz, dx)
        await_block(at, buf.at[at.r, slot], l_send.at[dz, dx], l_recv.at[slot])
    block = buf.at[at.r]
    for dy, dc in at.req_peers():
        sent.append(
            push(block, block, m_send.at[dy, dc], m_recv.at[at.r], at.req(dy, dc), at.u)
        )
    return sent


def end_packed(at, buf, send, recv):
    for dy, dc in at.req_peers():
        slot = at.req_from(dy, dc)
        await_block(at, buf.at[slot], send.at[dy, dc], recv.at[slot])


def pack_rows(accepted_ref, values):
    tree, depth = values.shape
    width = depth // PACK
    row = lax.broadcasted_iota(jnp.int32, (PACK * ACC, tree), 0)
    node = lax.broadcasted_iota(jnp.int32, (PACK * ACC, tree), 1)
    packed = jnp.zeros((PACK * ACC, width), jnp.float32)
    for chunk in range(PACK):
        pick = jnp.zeros((PACK * ACC, tree), jnp.float32)
        for i in range(ACC):
            hit = (row == chunk * ACC + i) & (node == accepted_ref[0, i])
            pick = jnp.where(hit, 1.0, pick)
        packed = packed + jnp.dot(
            pick.astype(jnp.bfloat16),
            values[:, chunk * width : (chunk + 1) * width],
            preferred_element_type=jnp.float32,
        )
    return packed


def packed_places(rows, chunk):
    shape = (rows, rows * PACK)
    row = lax.broadcasted_iota(jnp.int32, shape, 0)
    place = lax.broadcasted_iota(jnp.int32, shape, 1)
    base = row // ACC * (PACK * ACC) + lax.rem(row, ACC)
    return jnp.where(place == base + chunk * ACC, 1.0, 0.0).astype(jnp.bfloat16)


def unpack_rows(buf, every):
    reqs, units, packed, wide = buf.shape
    rows = units * ACC
    for k in range(reqs):
        flat = buf[k].reshape(units * packed, wide)
        for chunk in range(PACK):
            every[k * rows : (k + 1) * rows, chunk * wide : (chunk + 1) * wide] = jnp.dot(
                packed_places(rows, chunk), flat, preferred_element_type=jnp.float32
            ).astype(jnp.bfloat16)


def packed_rms(values, gain):
    width = values.shape[1]
    squares = jnp.sum(values * values, axis=1, keepdims=True)
    total = squares[:ACC]
    for chunk in range(1, PACK):
        total = total + squares[chunk * ACC : (chunk + 1) * ACC]
    factor = lax.rsqrt(total / (PACK * width) + EPS)
    gains = [
        jnp.broadcast_to(gain[:, chunk * width : (chunk + 1) * width], (ACC, width))
        for chunk in range(PACK)
    ]
    return (
        values
        * jnp.concatenate([factor] * PACK, axis=0)
        * jnp.concatenate(gains, axis=0).astype(jnp.float32)
    )


def layer_kernel(
    accepted_ref,
    attended_ref,
    hidden_ref,
    out_weight_ref,
    gains_ref,
    mlp_ref,
    draft_ref,
    tree_out_ref,
    drafts_ref,
    weights,
    attended_all,
    proj_send,
    proj_recv,
    first_ref,
    normed_ref,
    normed_all,
    part,
    sums_fast,
    sums_slow,
    own_sem,
    w_send,
    w_recv,
    a_send,
    a_recv,
    p_send,
    p_recv,
    n_send,
    n_recv,
    f_send,
    f_recv,
    s_send,
    s_recv,
    pack_one,
    paths_one,
    pack_two,
    paths_two,
    every,
    path_part,
    path_req,
    path_units,
    path_in,
    draft_weight,
    drafts,
    draft_sem,
    l1_send,
    l1_recv,
    m1_send,
    m1_recv,
    l2_send,
    l2_recv,
    m2_send,
    m2_recv,
    e_send,
    e_recv,
    g_send,
    g_recv,
    h_send,
    h_recv,
    q_send,
    q_recv,
    out_sem,
):
    at = Place()
    units, tree, depth = attended_all.shape
    matrices = mlp_ref.shape[0]
    reqs = at.reqs
    heads = draft_ref.shape[0]
    attn_gain, pre_gain = gains_ref[0:1, :], gains_ref[1:2, :]
    post_gain, final_gain = gains_ref[2:3, :], gains_ref[3:4, :]
    draft_load = pltpu.make_async_copy(
        draft_ref.at[at.r * heads // reqs], draft_weight, draft_sem
    )
    draft_load.start()
    meet(at)

    own_copy = pltpu.make_async_copy(mlp_ref, weights.at[at.r], own_sem)
    own_copy.start()
    w_sent = []

    def send_weights(m):
        for dy in range(1, at.chips):
            w_sent.append(
                push(
                    mlp_ref.at[m],
                    weights.at[at.r, m],
                    w_send.at[dy, 0, m],
                    w_recv.at[at.r, m],
                    at.req(dy, 0),
                    at.u,
                )
            )
        w_sent.append(
            push(
                mlp_ref.at[m],
                weights.at[at.r, m],
                w_send.at[0, 1, m],
                w_recv.at[at.r, m],
                at.req(0, 1),
                at.u,
            )
        )

    for m in range(matrices - 1):
        send_weights(m)

    def pass_on(m):
        for dy in range(1, at.chips):
            slot = at.req_from(dy, 0)
            block = weights.at[slot, m]
            await_block(at, block, w_send.at[dy, 0, m], w_recv.at[slot, m])
            w_sent.append(
                push(block, block, w_send.at[dy, 1, m], w_recv.at[slot, m], at.req(0, 1), at.u)
            )

    a_sent = start_gather(at, attended_ref, attended_all, a_send, a_recv)
    a_sent += forward_gather(at, attended_all, a_send, a_recv)
    sent = []
    end_gather(at, attended_all, a_send, a_recv)
    columns = jnp.dot(
        attended_all[...].reshape(units * tree, depth),
        out_weight_ref[...],
        preferred_element_type=jnp.float32,
    ).astype(jnp.bfloat16)
    proj_send[...] = columns.reshape(proj_send.shape)
    for dz, dx in at.unit_peers():
        peer = at.unit(dz, dx)
        sent.append(
            push(
                proj_send.at[peer],
                proj_recv.at[at.u],
                p_send.at[dz, dx],
                p_recv.at[at.u],
                at.r,
                peer,
            )
        )
    proj_recv[at.u] = proj_send[at.u]
    for dz, dx in at.unit_peers():
        slot = at.unit_from(dz, dx)
        await_block(at, proj_recv.at[slot], p_send.at[dz, dx], p_recv.at[slot])
    projected = jnp.concatenate([proj_recv[j] for j in range(units)], axis=1)
    first = (
        hidden_ref[...].astype(jnp.float32) + rms_scale(projected, attn_gain)
    ).astype(jnp.bfloat16)
    first_ref[...] = first
    normed = rms_scale(first, pre_gain).astype(jnp.bfloat16)
    normed_ref[...] = normed

    pack_one[...] = pack_rows(accepted_ref, normed).astype(jnp.bfloat16)
    path_first = pack_rows(accepted_ref, first)
    sent += start_packed(at, pack_one, paths_one, l1_send, l1_recv)
    sent += start_gather(at, normed_ref, normed_all, n_send, n_recv)
    sent += spread_packed(at, paths_one, l1_send, l1_recv, m1_send, m1_recv)
    send_weights(matrices - 1)
    pass_on(0)
    sent += forward_gather(at, normed_all, n_send, n_recv)
    for m in range(1, matrices - 1):
        pass_on(m)
    end_packed(at, paths_one, m1_send, m1_recv)
    unpack_rows(paths_one, every)
    own_copy.wait()
    rows, width = every.shape[0], depth // PACK
    gate = jnp.dot(every[...], weights[at.r, 0], preferred_element_type=jnp.float32)
    upward = jnp.dot(every[...], weights[at.r, 1], preferred_element_type=jnp.float32)
    active = (jax.nn.gelu(gate, approximate=True) * upward).astype(jnp.bfloat16)
    terms = [
        dot_nt(active, weights[at.r, 2, chunk * width : (chunk + 1) * width, :]).astype(
            jnp.bfloat16
        )
        for chunk in range(PACK)
    ]
    group = units * ACC
    for k in range(reqs):
        packed = jnp.zeros((group * PACK, width), jnp.float32)
        for chunk in range(PACK):
            packed = packed + lax.dot_general(
                packed_places(group, chunk),
                terms[chunk][k * group : (k + 1) * group, :],
                (((0,), (0,)), ((), ())),
                preferred_element_type=jnp.float32,
            )
        path_part[k] = packed.astype(jnp.bfloat16).reshape(path_part.shape[1:])

    def add_units(slot, start):
        rows = normed_all[...].reshape(units * tree, depth)
        gate = jnp.dot(rows, weights[slot, 0], preferred_element_type=jnp.float32)
        upward = jnp.dot(rows, weights[slot, 1], preferred_element_type=jnp.float32)
        active = (jax.nn.gelu(gate, approximate=True) * upward).astype(jnp.bfloat16)
        for chunk in range(PACK):
            span = slice(chunk * width, (chunk + 1) * width)
            terms = dot_nt(active, weights[slot, 2, span, :]).reshape(units, tree, width)
            part[:, :, span] = terms if start else part[:, :, span] + terms

    queue = [(dy, dc) for dy in range(at.chips) for dc in range(2)]

    def next_units():
        dy, dc = queue.pop(0)
        slot = at.req_from(dy, dc)
        if dc:
            for m in range(matrices):
                await_block(at, weights.at[slot, m], w_send.at[0, 1, m], w_recv.at[slot, m])
        add_units(slot if dy or dc else at.r, not (dy or dc))

    def end_units():
        while queue:
            next_units()

    for dy, dc in at.req_peers():
        peer = at.req(dy, dc)
        sent.append(
            push(
                path_part.at[peer],
                path_req.at[at.r],
                e_send.at[dy, dc],
                e_recv.at[at.r],
                peer,
                at.u,
            )
        )
    path_req[at.r] = path_part[at.r]
    end_gather(at, normed_all, n_send, n_recv)
    next_units()
    pass_on(matrices - 1)
    for dy, dc in at.req_peers():
        slot = at.req_from(dy, dc)
        await_block(at, path_req.at[slot], e_send.at[dy, dc], e_recv.at[slot])
    path_units[...] = jnp.sum(path_req[...].astype(jnp.float32), axis=0).astype(jnp.bfloat16)
    for dz, dx in at.unit_peers():
        peer = at.unit(dz, dx)
        sent.append(
            push(
                path_units.at[peer],
                path_in.at[at.u],
                g_send.at[dz, dx],
                g_recv.at[at.u],
                at.r,
                peer,
            )
        )
    path_in[at.u] = path_units[at.u]
    next_units()
    for dz, dx in at.unit_peers():
        slot = at.unit_from(dz, dx)
        await_block(at, path_in.at[slot], g_send.at[dz, dx], g_recv.at[slot])
    path_sum = jnp.sum(path_in[...].astype(jnp.float32), axis=0)
    path_out = (path_first + packed_rms(path_sum, post_gain)).astype(jnp.bfloat16)
    pack_two[...] = packed_rms(path_out.astype(jnp.float32), final_gain).astype(jnp.bfloat16)
    sent += start_packed(at, pack_two, paths_two, l2_send, l2_recv)
    sent += spread_packed(at, paths_two, l2_send, l2_recv, m2_send, m2_recv)
    next_units()
    end_packed(at, paths_two, m2_send, m2_recv)
    unpack_rows(paths_two, every)

    draft_load.wait()
    share, columns_here = drafts.shape[2:]
    if share == rows:
        mine = every.at[:, :]
    else:
        start = pl.multiple_of(lax.rem(at.r * share, rows), share)
        mine = every.at[pl.ds(start, share), :]
    before = jnp.dot(mine[...], draft_weight[...], preferred_element_type=jnp.float32)
    column = pl.multiple_of(at.u * columns_here, columns_here)
    own = mine[:, pl.ds(column, columns_here)].astype(jnp.float32)
    drafts[at.r, at.u] = (own + before * jax.nn.sigmoid(before)).astype(jnp.bfloat16)

    block = drafts.at[at.r, at.u]
    for dz in range(1, at.slow):
        sent.append(push(block, block, h_send.at[dz, 0], h_recv.at[at.u], at.r, at.unit(dz, 0)))
    for dx in range(1, at.fast):
        sent.append(push(block, block, h_send.at[0, dx], h_recv.at[at.u], at.r, at.unit(0, dx)))
    sent += forward_gather(at, drafts.at[at.r], h_send, h_recv)
    end_gather(at, drafts.at[at.r], h_send, h_recv)
    block = drafts.at[at.r]
    for dy in range(1, at.chips):
        sent.append(push(block, block, q_send.at[dy, 0], q_recv.at[at.r], at.req(dy, 0), at.u))
    sent.append(push(block, block, q_send.at[0, 1], q_recv.at[at.r], at.req(0, 1), at.u))

    end_units()

    for copy in a_sent:
        copy.wait_send()
    sums_send = attended_all
    order = list(range(1, at.slow)) + [0]
    for dz in order:
        for dx in range(1, at.fast):
            peer = at.unit(dz, dx)
            zt = peer // at.fast
            sums_send[peer] = part[peer].astype(jnp.bfloat16)
            sent.append(
                push(
                    sums_send.at[peer],
                    sums_fast.at[zt, at.x],
                    f_send.at[dz, dx],
                    f_recv.at[zt, at.x],
                    at.r,
                    at.unit(0, dx),
                )
            )
    for dy in range(1, at.chips):
        slot = at.req_from(dy, 0)
        block = drafts.at[slot]
        await_block(at, block, q_send.at[dy, 0], q_recv.at[slot])
        sent.append(push(block, block, q_send.at[dy, 1], q_recv.at[slot], at.req(0, 1), at.u))

    for dz in order:
        target = at.unit(dz, 0)
        zt = target // at.fast
        total = part[target]
        for dx in range(1, at.fast):
            xs = lax.rem(at.x + at.fast - dx, at.fast)
            await_block(at, sums_fast.at[zt, xs], f_send.at[dz, dx], f_recv.at[zt, xs])
            total = total + sums_fast[zt, xs].astype(jnp.float32)
        if dz:
            sums_send[target] = total.astype(jnp.bfloat16)
            sent.append(
                push(
                    sums_send.at[target],
                    sums_slow.at[at.z],
                    s_send.at[dz],
                    s_recv.at[at.z],
                    at.r,
                    target,
                )
            )
    for dz in range(1, at.slow):
        zs = lax.rem(at.z + at.slow - dz, at.slow)
        await_block(at, sums_slow.at[zs], s_send.at[dz], s_recv.at[zs])
        total = total + sums_slow[zs].astype(jnp.float32)
    tree_out_ref[...] = (
        first_ref[...].astype(jnp.float32) + rms_scale(total, post_gain)
    ).astype(jnp.bfloat16)
    for dy in range(at.chips):
        slot = at.req_from(dy, 1)
        await_block(at, drafts.at[slot], q_send.at[dy, 1], q_recv.at[slot])
    stores = [
        pltpu.make_async_copy(
            drafts.at[k, j],
            drafts_ref.at[
                k * share : (k + 1) * share, j * columns_here : (j + 1) * columns_here
            ],
            out_sem.at[k, j],
        )
        for k in range(reqs)
        for j in range(units)
    ]
    for store in stores:
        store.start()
    for store in stores:
        store.wait()
    for copy in sent + w_sent:
        copy.wait_send()


def layer(attended, hidden, accepted, out_weight, mlp_weights, draft_weights, gains):
    reqs, units = lax.axis_size("req"), lax.axis_size("unit")
    slow, fast = split_unit(units)
    tree, depth = hidden.shape
    bf16, dma = jnp.bfloat16, pltpu.SemaphoreType.DMA
    vmem = pl.BlockSpec(memory_space=pltpu.VMEM)
    rows = (units, tree, depth)
    cols = (units, tree, out_weight.shape[1])
    matrices, _, width = mlp_weights.shape
    heads, _, draft_width = draft_weights.shape
    path_rows = reqs * units * ACC
    block = (PACK * ACC, depth // PACK)
    share = heads * path_rows // reqs
    return pl.pallas_call(
        layer_kernel,
        out_shape=(
            jax.ShapeDtypeStruct((tree, depth), bf16),
            jax.ShapeDtypeStruct((heads * path_rows, depth), bf16),
        ),
        in_specs=[pl.BlockSpec(memory_space=pltpu.SMEM)]
        + [vmem] * 4
        + [pl.BlockSpec(memory_space=pl.ANY)] * 2,
        out_specs=(vmem, pl.BlockSpec(memory_space=pl.ANY)),
        scratch_shapes=[
            pltpu.VMEM((reqs, matrices, depth, width), bf16),
            pltpu.VMEM(rows, bf16),
            pltpu.VMEM(cols, bf16),
            pltpu.VMEM(cols, bf16),
            pltpu.VMEM((tree, depth), bf16),
            pltpu.VMEM((tree, depth), bf16),
            pltpu.VMEM(rows, bf16),
            pltpu.VMEM(rows, jnp.float32),
            pltpu.VMEM((slow, fast, tree, depth), bf16),
            pltpu.VMEM((slow, tree, depth), bf16),
            dma(()),
            dma((reqs // 2, 2, matrices)),
            dma((reqs, matrices)),
            dma((slow, fast)),
            dma((units,)),
            dma((slow, fast)),
            dma((units,)),
            dma((slow, fast)),
            dma((units,)),
            dma((slow, fast)),
            dma((slow, fast)),
            dma((slow,)),
            dma((slow,)),
            pltpu.VMEM(block, bf16),
            pltpu.VMEM((reqs, units) + block, bf16),
            pltpu.VMEM(block, bf16),
            pltpu.VMEM((reqs, units) + block, bf16),
            pltpu.VMEM((path_rows, depth), bf16),
            pltpu.VMEM((reqs, units) + block, bf16),
            pltpu.VMEM((reqs, units) + block, bf16),
            pltpu.VMEM((units,) + block, bf16),
            pltpu.VMEM((units,) + block, bf16),
            pltpu.VMEM((depth, draft_width), bf16),
            pltpu.VMEM((reqs, units, share, draft_width), bf16),
            dma(()),
            dma((slow, fast)),
            dma((units,)),
            dma((reqs // 2, 2)),
            dma((reqs,)),
            dma((slow, fast)),
            dma((units,)),
            dma((reqs // 2, 2)),
            dma((reqs,)),
            dma((reqs // 2, 2)),
            dma((reqs,)),
            dma((slow, fast)),
            dma((units,)),
            dma((slow, fast)),
            dma((units,)),
            dma((reqs // 2, 2)),
            dma((reqs,)),
            dma((reqs, units)),
        ],
        compiler_params=pltpu.CompilerParams(
            collective_id=0, has_side_effects=True, vmem_limit_bytes=56 * MIB
        ),
        name="projection_feed_forward_drafts",
    )(accepted, attended, hidden, out_weight, jnp.stack(gains), mlp_weights, draft_weights)


def sum_kernel(own_ref, out_ref, unit_parts, group, req_parts, u_send, u_recv, r_send, r_recv):
    at = Place()
    meet(at)
    sent = []
    for dz, dx in at.unit_peers():
        sent.append(
            push(
                own_ref,
                unit_parts.at[at.u],
                u_send.at[dz, dx],
                u_recv.at[at.u],
                at.r,
                at.unit(dz, dx),
            )
        )
    unit_parts[at.u] = own_ref[...]
    for dz, dx in at.unit_peers():
        slot = at.unit_from(dz, dx)
        await_block(at, unit_parts.at[slot], u_send.at[dz, dx], u_recv.at[slot])
    group[...] = jnp.sum(unit_parts[...], axis=0)
    for dy, dc in at.req_peers():
        sent.append(
            push(
                group,
                req_parts.at[at.r],
                r_send.at[dy, dc],
                r_recv.at[at.r],
                at.req(dy, dc),
                at.u,
            )
        )
    req_parts[at.r] = group[...]
    for dy, dc in at.req_peers():
        slot = at.req_from(dy, dc)
        await_block(at, req_parts.at[slot], r_send.at[dy, dc], r_recv.at[slot])
    out_ref[...] = jnp.sum(req_parts[...], axis=0)
    for copy in sent:
        copy.wait_send()


def sum_over_devices(values):
    reqs, units = lax.axis_size("req"), lax.axis_size("unit")
    slow, fast = split_unit(units)
    lines = max(8, values.shape[0] // 128)
    block = (lines, 128)
    f32, dma = jnp.float32, pltpu.SemaphoreType.DMA
    vmem = pl.BlockSpec(memory_space=pltpu.VMEM)
    padded = jnp.pad(values, (0, lines * 128 - values.shape[0])).reshape(block)
    summed = pl.pallas_call(
        sum_kernel,
        out_shape=jax.ShapeDtypeStruct(block, f32),
        in_specs=[vmem],
        out_specs=vmem,
        scratch_shapes=[
            pltpu.VMEM((units,) + block, f32),
            pltpu.VMEM(block, f32),
            pltpu.VMEM((reqs,) + block, f32),
            dma((slow, fast)),
            dma((units,)),
            dma((reqs // 2, 2)),
            dma((reqs,)),
        ],
        compiler_params=pltpu.CompilerParams(collective_id=2, has_side_effects=True),
        name="sum_of_totals",
    )(padded)
    return summed.reshape(-1)[: values.shape[0]]


def allowed_ids(start, end, first_id, shape):
    ids = first_id + lax.broadcasted_iota(jnp.int32, shape, 1)
    return (ids >= start) & (ids < end)


def logits_kernel(chunk, drafts_ref, emb_ref, start_ref, end_ref, logits_ref, sums_ref):
    step = pl.program_id(0)
    count = drafts_ref.shape[0]
    tile = emb_ref.shape[0]
    vocab = tile * pl.num_programs(0)
    first_id = (lax.axis_index("req") * lax.axis_size("unit") + lax.axis_index("unit")) * vocab

    @pl.when(step == 0)
    def _():
        sums_ref[...] = jnp.zeros_like(sums_ref)

    start, end = start_ref[...], end_ref[...]
    for c in range(tile // chunk):
        span = slice(c * chunk, (c + 1) * chunk)
        products = dot_nt(drafts_ref[...], emb_ref[span, :])
        logits = SOFTCAP * jnp.tanh(products * (1.0 / SOFTCAP))
        logits_ref[:, span] = logits.astype(jnp.bfloat16)
        keep = allowed_ids(start, end, first_id + step * tile + c * chunk, logits.shape)
        terms = jnp.where(keep, jnp.exp(logits), 0.0)
        part = terms[:, :128]
        for lane in range(128, chunk, 128):
            part = part + terms[:, lane : lane + 128]
        sums_ref[...] += part


def finish_kernel(logits_ref, logs_ref, start_ref, end_ref, out_ref):
    tile = logits_ref.shape[1]
    vocab = tile * pl.num_programs(0)
    first_id = (lax.axis_index("req") * lax.axis_size("unit") + lax.axis_index("unit")) * vocab
    keep = allowed_ids(
        start_ref[...], end_ref[...], first_id + pl.program_id(0) * tile, logits_ref.shape
    )
    values = jnp.where(keep, logits_ref[...].astype(jnp.float32) - logs_ref[...], 0.0).astype(jnp.bfloat16)
    out_ref[...] = values.reshape(out_ref.shape)


def vocabulary(drafts, embedding, tenant_ranges):
    count = drafts.shape[0]
    vocab, depth = embedding.shape
    rows = count // HEADS
    bounds = jnp.tile(jnp.repeat(tenant_ranges, ACC, axis=0), (HEADS, 1))
    starts, ends = bounds[:, :1], bounds[:, 1:]
    tile = min(1024, vocab, MIB // 2 // count)
    once = pl.BlockSpec((count, 1), lambda i: (0, 0))
    logits, sums = pl.pallas_call(
        functools.partial(logits_kernel, min(256, tile)),
        grid=(vocab // tile,),
        out_shape=(
            jax.ShapeDtypeStruct((count, vocab), jnp.bfloat16),
            jax.ShapeDtypeStruct((count, 128), jnp.float32),
        ),
        in_specs=[
            pl.BlockSpec((count, depth), lambda i: (0, 0)),
            pl.BlockSpec((tile, depth), lambda i: (i, 0)),
            once,
            once,
        ],
        out_specs=(
            pl.BlockSpec((count, tile), lambda i: (0, i)),
            pl.BlockSpec((count, 128), lambda i: (0, 0)),
        ),
        compiler_params=pltpu.CompilerParams(vmem_limit_bytes=56 * MIB),
        cost_estimate=pl.CostEstimate(
            flops=2 * count * depth * vocab,
            bytes_accessed=2 * depth * vocab + 2 * count * vocab,
            transcendentals=2 * count * vocab,
        ),
        name="vocabulary_logits",
    )(drafts, embedding, starts, ends)
    totals = sum_over_devices(jnp.sum(sums, axis=1))
    return pl.pallas_call(
        finish_kernel,
        grid=(vocab // tile,),
        out_shape=jax.ShapeDtypeStruct((HEADS, rows, vocab), jnp.bfloat16),
        in_specs=[pl.BlockSpec((count, tile), lambda i: (0, i)), once, once, once],
        out_specs=pl.BlockSpec((HEADS, rows, tile), lambda i: (0, 0, i)),
        compiler_params=pltpu.CompilerParams(vmem_limit_bytes=40 * MIB),
        cost_estimate=pl.CostEstimate(
            flops=2 * count * vocab, bytes_accessed=4 * count * vocab, transcendentals=0
        ),
        name="log_probabilities",
    )(logits, jnp.log(totals)[:, None], starts, ends)


def per_device(
    hidden,
    tree_q,
    tree_kv,
    kv_cache,
    cache_lengths,
    tree_parents,
    accepted,
    tenant_ranges,
    out_weight,
    mlp_weights,
    draft_weights,
    embedding,
    attn_post_gain,
    ff_pre_gain,
    ff_post_gain,
    final_gain,
):
    attended = attend(tree_q, tree_kv, kv_cache, cache_lengths, tree_parents)
    gains = (attn_post_gain, ff_pre_gain, ff_post_gain, final_gain)
    tree_out, drafts = layer(
        attended, hidden, accepted, out_weight, mlp_weights, draft_weights, gains
    )
    return (tree_out, vocabulary(drafts, embedding, tenant_ranges))


def solution(mesh):
    return jax.shard_map(
        per_device,
        mesh=mesh,
        in_specs=(
            P(("req", "unit"), None),
            P(("req", "unit"), None),
            P(("req", "unit"), None, None),
            P(("req", "unit"), None, None, None, None),
            P(("req", "unit")),
            P(("req", "unit"), None),
            P(("req", "unit"), None),
            P(),
            P(None, "unit"),
            P(None, None, ("req", "unit")),
            P(None, None, "unit"),
            P(("req", "unit"), None),
            P(),
            P(),
            P(),
            P(),
        ),
        out_specs=(P(("req", "unit"), None), P(None, None, ("req", "unit"))),
        check_vma=False,
    )
```
